32 devices in a mesh: band: 2 (over y), dom: 16 (over z, x, core).
Axes of the slice: x: 2, y: 2, z: 4, core: 2. Of those that a mesh axis runs over, the one named last changes fastest.
Arguments:
- orbitals: bfloat16 [512, 32, 32, 128], P('band', 'dom'), may hold values from -270 to 270
- potential: float32 [32, 32, 128], P('dom'), may hold values from 0 to 4
Outputs:
- rotated: bfloat16 [512, 32, 32, 128], P('band', 'dom')
The draws below stay inside these ranges and needn't reach their ends.
All inputs are finite; a program needn't handle non-finite values.
Results may differ from the reference program's by a relative error of at most 0.025.
Values may be sent and summed in bfloat16 or wider, within the bound.
A program may use at most 128 MiB of HBM per device.

```python
import math
from functools import partial
import jax
import jax.numpy as jnp
from jax import lax

NORB = 512
NY = 32
NZ = 128
NX = 32


def draw_orbitals(key, part):
    key = jax.random.fold_in(key, 11)
    key_noise, key_shared, key_weight, key_scale = jax.random.split(key, 4)
    position = jnp.arange(NX, dtype=jnp.float32) / max(NX - 1, 1)
    noise = jax.random.truncated_normal(key_noise, -5.0, 5.0, (NORB, NX, NY, NZ), jnp.float32)
    shared = jax.random.truncated_normal(key_shared, -5.0, 5.0, (1, NX, NY, NZ), jnp.float32)
    envelope = 1.0 + 2.0 * position
    weights = jax.random.uniform(key_weight, (NORB, 1, 1, 1), jnp.float32, 0.3, 0.8)
    scales = jnp.exp(jax.random.uniform(key_scale, (NORB, 1, 1, 1), jnp.float32, 0.0, math.log(10.0)))
    return (scales * envelope[None, :, None, None] * (noise + weights * shared)).astype(jnp.bfloat16)


def block_levels(stream_key, extent, cuts, least, largest):
    factor_of, own = 1.0, jax.random.fold_in(stream_key, 6)
    for dim, shards_of in cuts:
        heights = jnp.exp(jax.random.uniform(jax.random.fold_in(own, dim), (shards_of,), jnp.float32, least / len(cuts), largest / len(cuts)))
        factor_of = factor_of * jnp.repeat(heights, extent[dim] // shards_of).reshape([-1 if axis == dim else 1 for axis in range(len(extent))])
    return factor_of


def setup_inputs(seed: int = 0) -> dict:
    key_of = jax.random.split(jax.random.key(seed), 3)
    return {
        "orbitals": draw_orbitals(jax.random.fold_in(key_of[2], 71), 0),
        "potential": jnp.clip(4.0 * jax.random.uniform(key_of[1], (NX, NY, NZ), jnp.float32) ** block_levels(key_of[1], (NX, NY, NZ), ((0, 16),), -0.2, 0.2), 0.0, 4.0),
    }


spectrum_center = 7.5
spectrum_half = 4.5

def neighbours(padded, axis_dim, offset):
    index_list = [slice(None), slice(2, -2), slice(2, -2), slice(2, -2)]
    index_list[axis_dim] = slice(2 + offset, padded.shape[axis_dim] - 2 + offset)
    return padded[tuple(index_list)]

def hamiltonian(padded, potential):
    center = neighbours(padded, 1, 0)
    laplace = -7.5 * center
    for axis_dim in (1, 2, 3):
        near_sum = neighbours(padded, axis_dim, 1) + neighbours(padded, axis_dim, -1)
        far_sum = neighbours(padded, axis_dim, 2) + neighbours(padded, axis_dim, -2)
        laplace = laplace + 4.0 / 3.0 * near_sum - 1.0 / 12.0 * far_sum
    return (-0.5 * laplace + potential * center, center)

def chebyshev(field, operate):
    image, anchor = operate(field)
    degree_one = ((image - spectrum_center * anchor) / spectrum_half).astype(jnp.bfloat16)
    image, current = operate(degree_one)
    second = (2.0 * (image - spectrum_center * current) / spectrum_half - anchor).astype(jnp.bfloat16)
    image, latest = operate(second)
    return (2.0 * (image - spectrum_center * latest) / spectrum_half - current).astype(jnp.bfloat16)

def local_operator(field, potential):
    padded = jnp.pad(field.astype(jnp.float32), ((0, 0), (2, 2), (2, 2), (2, 2)))
    return hamiltonian(padded, potential)

def reference(orbitals, potential):
    grouped = orbitals.reshape(NORB // 8, 8, NX, NY, NZ)
    operate = partial(local_operator, potential=potential)
    filtered = lax.map(lambda orbital_group: chebyshev(orbital_group, operate), grouped)
    flat = filtered.reshape(NORB, NX * NY * NZ)
    gram = lax.dot_general(flat.astype(jnp.float32), flat.astype(jnp.float32), (((1,), (1,)), ((), ())), preferred_element_type=jnp.float32) / (NX * NY * NZ)
    factor = jnp.linalg.cholesky(gram)
    inverse_factor = lax.linalg.triangular_solve(factor, jnp.eye(NORB, dtype=jnp.float32), left_side=True, lower=True)
    rotation = inverse_factor.astype(jnp.bfloat16)
    rotated = jnp.dot(rotation.astype(jnp.float32), flat.astype(jnp.float32), preferred_element_type=jnp.float32).astype(jnp.bfloat16)
    return rotated.reshape(NORB, NX, NY, NZ)
```

```python
import functools

import jax
import jax.numpy as jnp
import numpy as np
from jax import lax
from jax.experimental import pallas as pl
from jax.experimental.pallas import tpu as pltpu
from jax.sharding import PartitionSpec as P

MESH = pl.DeviceIdType.MESH
spectrum_center = 7.5
spectrum_half = 4.5
GROUP = 4
CHUNK = 16


def band_matrix(blocks, size):
    one = 16.0 * (np.eye(size, k=1) + np.eye(size, k=-1)) - np.eye(size, k=2) - np.eye(size, k=-2)
    return jnp.asarray(np.kron(np.eye(blocks), one), jnp.bfloat16)


def filter_kernel(
    bands, doms, orb_ref, pot_ref, ty_ref, tz_ref, gram_ref, held_ref,
    f0, f1, f2, pot, wide, sent, held,
    in_send, in_recv, pot_send, pot_recv, halo_send, halo_recv, out_send, out_recv, own_sem,
):
    orbs, planes, ny, nz = orb_ref.shape
    share = orbs // GROUP
    slab = GROUP * planes
    chunks = share // CHUNK
    rows_dev = planes * ny
    rows_part = rows_dev // bands
    b, d = lax.axis_index("band"), lax.axis_index("dom")
    g, z = lax.rem(d, GROUP), d // GROUP
    z_count = doms // GROUP
    base = z * GROUP
    has_low, has_high = z > 0, z < z_count - 1

    def peer(k, j=0):
        return (lax.rem(b + j, bands), base + lax.rem(g + k, GROUP))

    barrier = pltpu.get_barrier_semaphore()
    for k in range(GROUP):
        for j in range(bands):
            if k or j:
                pl.semaphore_signal(barrier, inc=1, device_id=peer(k, j), device_id_type=MESH)

    @pl.when(has_low)
    def _():
        pl.semaphore_signal(barrier, inc=1, device_id=(b, d - GROUP), device_id_type=MESH)

    @pl.when(has_high)
    def _():
        pl.semaphore_signal(barrier, inc=1, device_id=(b, d + GROUP), device_id_type=MESH)

    ends = jnp.where(has_low, 1, 0) + jnp.where(has_high, 1, 0)
    pl.semaphore_wait(barrier, GROUP * bands - 1 + ends)

    pot_copies, in_copies = [], {}
    own_planes = pl.ds(g * planes, planes)
    for k in range(1, GROUP):
        copy = pltpu.make_async_remote_copy(
            pot_ref, pot.at[own_planes], pot_send.at[k - 1], pot_recv.at[k - 1],
            device_id=peer(k), device_id_type=MESH,
        )
        copy.start()
        pot_copies.append(copy)
    own_pot = pltpu.make_async_copy(pot_ref, pot.at[own_planes], own_sem.at[chunks])
    own_pot.start()
    own_in = []
    for c in range(chunks):
        span = pl.ds(c * CHUNK, CHUNK)
        landing = f0.at[span, pl.ds(2 + g * planes, planes)]
        for k in range(1, GROUP):
            first = lax.rem(g + k, GROUP) * share + c * CHUNK
            copy = pltpu.make_async_remote_copy(
                orb_ref.at[pl.ds(first, CHUNK)], landing,
                in_send.at[c, k - 1], in_recv.at[c, k - 1],
                device_id=peer(k), device_id_type=MESH,
            )
            copy.start()
            in_copies[c, k] = copy
        copy = pltpu.make_async_copy(
            orb_ref.at[pl.ds(g * share + c * CHUNK, CHUNK)], landing, own_sem.at[c]
        )
        copy.start()
        own_in.append(copy)

    fields = (f0, f1, f2)

    @pl.when(jnp.logical_not(has_low))
    def _():
        for field in fields:
            field[:, 0:2] = jnp.zeros((share, 2, ny, nz), jnp.bfloat16)

    @pl.when(jnp.logical_not(has_high))
    def _():
        for field in fields:
            field[:, slab + 2 :] = jnp.zeros((share, 2, ny, nz), jnp.bfloat16)

    def halo(s, c):
        field, span = fields[s], pl.ds(c * CHUNK, CHUNK)
        down = pltpu.make_async_remote_copy(
            field.at[span, pl.ds(2, 2)], field.at[span, pl.ds(slab + 2, 2)],
            halo_send.at[s, c, 0], halo_recv.at[s, c, 0],
            device_id=(b, d - GROUP), device_id_type=MESH,
        )
        up = pltpu.make_async_remote_copy(
            field.at[span, pl.ds(slab, 2)], field.at[span, pl.ds(0, 2)],
            halo_send.at[s, c, 1], halo_recv.at[s, c, 1],
            device_id=(b, d + GROUP), device_id_type=MESH,
        )
        return down, up

    def send_halo(s, c):
        down, up = halo(s, c)
        pl.when(has_low)(down.start)
        pl.when(has_high)(up.start)

    def wait_halo(s, c):
        down, up = halo(s, c)
        pl.when(has_low)(up.wait_recv)
        pl.when(has_high)(down.wait_recv)

    def wait_halo_sent(s, c):
        down, up = halo(s, c)
        pl.when(has_low)(down.wait_send)
        pl.when(has_high)(up.wait_send)

    def apply(s, c):
        field = fields[s]
        factor = (1.0 if s == 0 else 2.0) / spectrum_half
        shift = 0.5 * 7.5 - spectrum_center

        def value(p, first):
            span = pl.ds(first, 8)

            def at(q):
                return field[span, q].reshape(8 * ny, nz)

            def wide_at(q):
                return at(q).astype(jnp.float32)

            v = at(p + 2)
            total = jnp.dot(ty_ref[...], v, preferred_element_type=jnp.float32)
            total += jnp.dot(v, tz_ref[...], preferred_element_type=jnp.float32)
            total += 16.0 * (wide_at(p + 1) + wide_at(p + 3)) - (wide_at(p) + wide_at(p + 4))
            scale = (pot[p] + shift) * factor
            own = (v.astype(jnp.float32).reshape(8, ny, nz) * scale[None]).reshape(8 * ny, nz)
            new = own - total * (factor / 24.0)
            if s > 0:
                old = fields[s - 1][span, p + 2].reshape(8 * ny, nz)
                new = new - old.astype(jnp.float32)
            return new

        if s < 2:
            def body(i, _):
                p, first = i // 2, pl.multiple_of(c * CHUNK + lax.rem(i, 2) * 8, 8)
                new = value(p, first).astype(jnp.bfloat16)
                fields[s + 1][pl.ds(first, 8), p + 2] = new.reshape(8, ny, nz)
                return 0

            lax.fori_loop(0, 2 * slab, body, 0)
        else:
            def body(p, _):
                for h in range(2):
                    wide[pl.ds(h * 8 * ny, 8 * ny), :] = value(p, c * CHUNK + h * 8)
                for y in range(ny):
                    rows = wide[pl.ds(y, CHUNK, stride=ny), :]
                    sent[c, p * ny + y] = rows.astype(jnp.bfloat16)
                return 0

            lax.fori_loop(0, slab, body, 0)

    own_out, out_copies = [], []

    def send_out(c):
        landing = held.at[(b * GROUP + g) * chunks + c]
        for k in range(GROUP):
            for j in range(bands):
                row = lax.rem(g + k, GROUP) * rows_dev + lax.rem(b + j, bands) * rows_part
                source = sent.at[c, pl.ds(row, rows_part)]
                if k or j:
                    at = k * bands + j - 1
                    copy = pltpu.make_async_remote_copy(
                        source, landing, out_send.at[c, at], out_recv.at[c, at],
                        device_id=peer(k, j), device_id_type=MESH,
                    )
                    out_copies.append(copy)
                else:
                    copy = pltpu.make_async_copy(source, landing, own_sem.at[chunks + 1 + c])
                    own_out.append(copy)
                copy.start()

    for copy in pot_copies:
        copy.wait_recv()
    own_pot.wait()
    for t in range(chunks + 3):
        if t < chunks:
            own_in[t].wait()
            for k in range(1, GROUP):
                in_copies[t, k].wait_recv()
            send_halo(0, t)
        for s in (2, 1, 0):
            c = t - 1 - s
            if 0 <= c < chunks:
                wait_halo(s, c)
                apply(s, c)
                if s < 2:
                    send_halo(s + 1, c)
                else:
                    send_out(c)

    for copy in own_out:
        copy.wait()
    for copy in out_copies:
        copy.wait_recv()
    keep = pltpu.make_async_copy(held, held_ref, own_sem.at[2 * chunks + 1])
    keep.start()

    everyone = bands * orbs
    step = min(8, rows_part)

    def terms(i, _):
        x = jnp.concatenate(
            [held[:, i * step + j].reshape(everyone, nz) for j in range(step)], axis=1
        )
        part = lax.dot_general(
            x, x, (((1,), (1,)), ((), ())), preferred_element_type=jnp.float32
        )
        gram_ref[...] += part
        return 0

    gram_ref[...] = jnp.zeros(gram_ref.shape, jnp.float32)
    lax.fori_loop(0, rows_part // step, terms, 0)

    for copy in pot_copies:
        copy.wait_send()
    for copy in in_copies.values():
        copy.wait_send()
    for s in range(3):
        for c in range(chunks):
            wait_halo_sent(s, c)
    for copy in out_copies:
        copy.wait_send()
    keep.wait()


def filter_and_gram(orbitals, potential, bands, doms):
    orbs, planes, ny, nz = orbitals.shape
    share, slab = orbs // GROUP, GROUP * planes
    chunks = share // CHUNK
    rows_part = planes * ny // bands
    held = (bands * orbs // CHUNK, rows_part, CHUNK, nz)
    field = pltpu.VMEM((share, slab + 4, ny, nz), jnp.bfloat16)
    others = GROUP * bands - 1
    dma = pltpu.SemaphoreType.DMA
    vmem = pl.BlockSpec(memory_space=pltpu.VMEM)
    hbm = pl.BlockSpec(memory_space=pl.ANY)
    return pl.pallas_call(
        functools.partial(filter_kernel, bands, doms),
        out_shape=(
            jax.ShapeDtypeStruct((bands * orbs, bands * orbs), jnp.float32),
            jax.ShapeDtypeStruct(held, jnp.bfloat16),
        ),
        in_specs=[hbm, vmem, vmem, vmem],
        out_specs=(vmem, hbm),
        scratch_shapes=[
            field, field, field,
            pltpu.VMEM((slab, ny, nz), jnp.float32),
            pltpu.VMEM((CHUNK * ny, nz), jnp.float32),
            pltpu.VMEM((chunks, slab * ny, CHUNK, nz), jnp.bfloat16),
            pltpu.VMEM(held, jnp.bfloat16),
            dma((chunks, GROUP - 1)), dma((chunks, GROUP - 1)),
            dma((GROUP - 1,)), dma((GROUP - 1,)),
            dma((3, chunks, 2)), dma((3, chunks, 2)),
            dma((chunks, others)), dma((chunks, others)),
            dma((2 * chunks + 2,)),
        ],
        compiler_params=pltpu.CompilerParams(
            collective_id=0, has_side_effects=True, vmem_limit_bytes=56 * 2**20
        ),
        name="filter_and_gram",
    )(orbitals, potential, band_matrix(8, ny), band_matrix(1, nz))


def rotate_kernel(own_ref, *refs):
    pieces, (first_ref, out_ref, wide) = refs[:-3], refs[-3:]
    count, rows, chunk, nz = pieces[0].shape
    orbs, all_rows = out_ref.shape[0], out_ref.shape[1]
    for j, piece in enumerate(pieces):
        start = first_ref[j]

        def body(i, _, piece=piece, start=start):
            x = jnp.concatenate(
                [piece[:, 2 * i + h].reshape(count * chunk, nz) for h in range(2)], axis=1
            )
            y = jnp.dot(own_ref[...], x, preferred_element_type=jnp.float32)
            for h in range(2):
                at = pl.ds(start + 2 * i + h, orbs, stride=all_rows)
                wide[at, :] = y[:, h * nz : (h + 1) * nz]
            return 0

        lax.fori_loop(0, rows // 2, body, 0)

    def narrow(i, _):
        part = wide[pl.ds(pl.multiple_of(i * 8 * all_rows, 8 * all_rows), 8 * all_rows), :]
        out_ref[pl.ds(i * 8, 8)] = part.reshape(8, all_rows, nz).astype(jnp.bfloat16)
        return 0

    lax.fori_loop(0, orbs // 8, narrow, 0)


def rotate(own_rows, pieces, firsts, all_rows):
    orbs = own_rows.shape[0]
    nz = pieces[0].shape[3]
    vmem = pl.BlockSpec(memory_space=pltpu.VMEM)
    return pl.pallas_call(
        rotate_kernel,
        out_shape=jax.ShapeDtypeStruct((orbs, all_rows, nz), jnp.bfloat16),
        in_specs=[vmem] * (1 + len(pieces)) + [pl.BlockSpec(memory_space=pltpu.SMEM)],
        out_specs=vmem,
        scratch_shapes=[pltpu.VMEM((orbs * all_rows, nz), jnp.float32)],
        compiler_params=pltpu.CompilerParams(vmem_limit_bytes=48 * 2**20),
        name="rotate",
    )(own_rows, *pieces, firsts)


def rotation_from(gram):
    factor = jnp.linalg.cholesky(gram)
    identity = jnp.eye(gram.shape[0], dtype=jnp.float32)
    inverse_factor = lax.linalg.triangular_solve(factor, identity, left_side=True, lower=True)
    return inverse_factor.astype(jnp.bfloat16)


def local(bands, doms, orbitals, potential):
    orbs, planes, ny, nz = orbitals.shape
    all_rows = planes * ny
    total_cells = all_rows * nz * doms
    part, held = filter_and_gram(orbitals, potential, bands, doms)
    pieces = [held]
    for j in range(1, bands):
        ring = [((i + j) % bands, i) for i in range(bands)]
        pieces.append(lax.ppermute(held, "band", ring))
    gram = lax.psum(part, ("band", "dom")) / total_cells
    rotation = rotation_from(gram)
    b = lax.axis_index("band")
    own_rows = lax.dynamic_slice_in_dim(rotation, b * orbs, orbs, 0)
    firsts = (b + jnp.arange(bands, dtype=jnp.int32)) % bands * (all_rows // bands)
    result = rotate(own_rows, pieces, firsts.astype(jnp.int32), all_rows)
    return result.reshape(orbitals.shape)


def solution(mesh):
    placed = (P("band", "dom", None, None), P("dom", None, None))
    return jax.shard_map(
        functools.partial(local, mesh.shape["band"], mesh.shape["dom"]),
        mesh=mesh, in_specs=placed, out_specs=P("band", "dom", None, None), check_vma=False,
    )
```

```python
import functools

import jax
import jax.numpy as jnp
import numpy as np
from jax import lax
from jax.experimental import pallas as pl
from jax.experimental.pallas import tpu as pltpu
from jax.sharding import PartitionSpec as P

MESH = pl.DeviceIdType.MESH
spectrum_center = 7.5
spectrum_half = 4.5
GROUP = 4
CHUNK = 16


def band_matrix(blocks, size):
    one = 16.0 * (np.eye(size, k=1) + np.eye(size, k=-1)) - np.eye(size, k=2) - np.eye(size, k=-2)
    return jnp.asarray(np.kron(np.eye(blocks), one), jnp.bfloat16)


def filter_kernel(
    bands, doms, orb_ref, pot_ref, ty_ref, tz_ref, gram_ref, held_ref,
    f0, f1, f2, pot, wide, sent, held,
    in_send, in_recv, pot_send, pot_recv, halo_send, halo_recv, out_send, out_recv, own_sem,
):
    orbs, planes, ny, nz = orb_ref.shape
    share = orbs // GROUP
    slab = GROUP * planes
    chunks = share // CHUNK
    rows_dev = planes * ny
    rows_part = rows_dev // bands
    b, d = lax.axis_index("band"), lax.axis_index("dom")
    g, z = lax.rem(d, GROUP), d // GROUP
    z_count = doms // GROUP
    base = z * GROUP
    has_low, has_high = z > 0, z < z_count - 1

    def peer(k, j=0):
        return (lax.rem(b + j, bands), base + lax.rem(g + k, GROUP))

    barrier = pltpu.get_barrier_semaphore()
    for k in range(GROUP):
        for j in range(bands):
            if k or j:
                pl.semaphore_signal(barrier, inc=1, device_id=peer(k, j), device_id_type=MESH)

    @pl.when(has_low)
    def _():
        pl.semaphore_signal(barrier, inc=1, device_id=(b, d - GROUP), device_id_type=MESH)

    @pl.when(has_high)
    def _():
        pl.semaphore_signal(barrier, inc=1, device_id=(b, d + GROUP), device_id_type=MESH)

    ends = jnp.where(has_low, 1, 0) + jnp.where(has_high, 1, 0)
    pl.semaphore_wait(barrier, GROUP * bands - 1 + ends)

    pot_copies, in_copies = [], {}
    own_planes = pl.ds(g * planes, planes)
    for k in range(1, GROUP):
        copy = pltpu.make_async_remote_copy(
            pot_ref, pot.at[own_planes], pot_send.at[k - 1], pot_recv.at[k - 1],
            device_id=peer(k), device_id_type=MESH,
        )
        copy.start()
        pot_copies.append(copy)
    own_pot = pltpu.make_async_copy(pot_ref, pot.at[own_planes], own_sem.at[chunks])
    own_pot.start()
    own_in = []
    for c in range(chunks):
        span = pl.ds(c * CHUNK, CHUNK)
        landing = f0.at[span, pl.ds(2 + g * planes, planes)]
        for k in range(1, GROUP):
            first = lax.rem(g + k, GROUP) * share + c * CHUNK
            copy = pltpu.make_async_remote_copy(
                orb_ref.at[pl.ds(first, CHUNK)], landing,
                in_send.at[c, k - 1], in_recv.at[c, k - 1],
                device_id=peer(k), device_id_type=MESH,
            )
            copy.start()
            in_copies[c, k] = copy
        copy = pltpu.make_async_copy(
            orb_ref.at[pl.ds(g * share + c * CHUNK, CHUNK)], landing, own_sem.at[c]
        )
        copy.start()
        own_in.append(copy)

    fields = (f0, f1, f2)

    @pl.when(jnp.logical_not(has_low))
    def _():
        for field in fields:
            field[:, 0:2] = jnp.zeros((share, 2, ny, nz), jnp.bfloat16)

    @pl.when(jnp.logical_not(has_high))
    def _():
        for field in fields:
            field[:, slab + 2 :] = jnp.zeros((share, 2, ny, nz), jnp.bfloat16)

    def halo(s, c):
        field, span = fields[s], pl.ds(c * CHUNK, CHUNK)
        down = pltpu.make_async_remote_copy(
            field.at[span, pl.ds(2, 2)], field.at[span, pl.ds(slab + 2, 2)],
            halo_send.at[s, c, 0], halo_recv.at[s, c, 0],
            device_id=(b, d - GROUP), device_id_type=MESH,
        )
        up = pltpu.make_async_remote_copy(
            field.at[span, pl.ds(slab, 2)], field.at[span, pl.ds(0, 2)],
            halo_send.at[s, c, 1], halo_recv.at[s, c, 1],
            device_id=(b, d + GROUP), device_id_type=MESH,
        )
        return down, up

    def send_halo(s, c):
        down, up = halo(s, c)
        pl.when(has_low)(down.start)
        pl.when(has_high)(up.start)

    def wait_halo(s, c):
        down, up = halo(s, c)
        pl.when(has_low)(up.wait_recv)
        pl.when(has_high)(down.wait_recv)

    def wait_halo_sent(s, c):
        down, up = halo(s, c)
        pl.when(has_low)(down.wait_send)
        pl.when(has_high)(up.wait_send)

    def apply(s, c):
        field = fields[s]
        factor = (1.0 if s == 0 else 2.0) / spectrum_half
        shift = 0.5 * 7.5 - spectrum_center

        def value(p, first):
            span = pl.ds(first, 8)

            def at(q):
                return field[span, q].reshape(8 * ny, nz)

            def wide_at(q):
                return at(q).astype(jnp.float32)

            v = at(p + 2)
            total = jnp.dot(ty_ref[...], v, preferred_element_type=jnp.float32)
            total += jnp.dot(v, tz_ref[...], preferred_element_type=jnp.float32)
            total += 16.0 * (wide_at(p + 1) + wide_at(p + 3)) - (wide_at(p) + wide_at(p + 4))
            scale = (pot[p] + shift) * factor
            own = (v.astype(jnp.float32).reshape(8, ny, nz) * scale[None]).reshape(8 * ny, nz)
            new = own - total * (factor / 24.0)
            if s > 0:
                old = fields[s - 1][span, p + 2].reshape(8 * ny, nz)
                new = new - old.astype(jnp.float32)
            return new

        if s < 2:
            def body(i, _):
                p, first = i // 2, pl.multiple_of(c * CHUNK + lax.rem(i, 2) * 8, 8)
                new = value(p, first).astype(jnp.bfloat16)
                fields[s + 1][pl.ds(first, 8), p + 2] = new.reshape(8, ny, nz)
                return 0

            lax.fori_loop(0, 2 * slab, body, 0)
        else:
            def body(p, _):
                for h in range(2):
                    wide[pl.ds(h * 8 * ny, 8 * ny), :] = value(p, c * CHUNK + h * 8)
                for y in range(ny):
                    rows = wide[pl.ds(y, CHUNK, stride=ny), :]
                    sent[c, p * ny + y] = rows.astype(jnp.bfloat16)
                return 0

            lax.fori_loop(0, slab, body, 0)

    own_out, out_copies = [], []

    def send_out(c):
        landing = held.at[(b * GROUP + g) * chunks + c]
        for k in range(GROUP):
            for j in range(bands):
                row = lax.rem(g + k, GROUP) * rows_dev + lax.rem(b + j, bands) * rows_part
                source = sent.at[c, pl.ds(row, rows_part)]
                if k or j:
                    at = k * bands + j - 1
                    copy = pltpu.make_async_remote_copy(
                        source, landing, out_send.at[c, at], out_recv.at[c, at],
                        device_id=peer(k, j), device_id_type=MESH,
                    )
                    out_copies.append(copy)
                else:
                    copy = pltpu.make_async_copy(source, landing, own_sem.at[chunks + 1 + c])
                    own_out.append(copy)
                copy.start()

    for copy in pot_copies:
        copy.wait_recv()
    own_pot.wait()
    for t in range(chunks + 3):
        if t < chunks:
            own_in[t].wait()
            for k in range(1, GROUP):
                in_copies[t, k].wait_recv()
            send_halo(0, t)
        for s in (2, 1, 0):
            c = t - 1 - s
            if 0 <= c < chunks:
                wait_halo(s, c)
                apply(s, c)
                if s < 2:
                    send_halo(s + 1, c)
                else:
                    send_out(c)

    for copy in own_out:
        copy.wait()
    for copy in out_copies:
        copy.wait_recv()
    keep = pltpu.make_async_copy(held, held_ref, own_sem.at[2 * chunks + 1])
    keep.start()

    everyone = bands * orbs
    step = min(8, rows_part)

    def terms(i, _):
        x = jnp.concatenate(
            [held[:, i * step + j].reshape(everyone, nz) for j in range(step)], axis=1
        )
        part = lax.dot_general(
            x, x, (((1,), (1,)), ((), ())), preferred_element_type=jnp.float32
        )
        gram_ref[...] += part
        return 0

    gram_ref[...] = jnp.zeros(gram_ref.shape, jnp.float32)
    lax.fori_loop(0, rows_part // step, terms, 0)

    for copy in pot_copies:
        copy.wait_send()
    for copy in in_copies.values():
        copy.wait_send()
    for s in range(3):
        for c in range(chunks):
            wait_halo_sent(s, c)
    for copy in out_copies:
        copy.wait_send()
    keep.wait()


def filter_and_gram(orbitals, potential, bands, doms):
    orbs, planes, ny, nz = orbitals.shape
    share, slab = orbs // GROUP, GROUP * planes
    chunks = share // CHUNK
    rows_part = planes * ny // bands
    held = (bands * orbs // CHUNK, rows_part, CHUNK, nz)
    field = pltpu.VMEM((share, slab + 4, ny, nz), jnp.bfloat16)
    others = GROUP * bands - 1
    dma = pltpu.SemaphoreType.DMA
    vmem = pl.BlockSpec(memory_space=pltpu.VMEM)
    hbm = pl.BlockSpec(memory_space=pl.ANY)
    return pl.pallas_call(
        functools.partial(filter_kernel, bands, doms),
        out_shape=(
            jax.ShapeDtypeStruct((bands * orbs, bands * orbs), jnp.float32),
            jax.ShapeDtypeStruct(held, jnp.bfloat16),
        ),
        in_specs=[hbm, vmem, vmem, vmem],
        out_specs=(vmem, hbm),
        scratch_shapes=[
            field, field, field,
            pltpu.VMEM((slab, ny, nz), jnp.float32),
            pltpu.VMEM((CHUNK * ny, nz), jnp.float32),
            pltpu.VMEM((chunks, slab * ny, CHUNK, nz), jnp.bfloat16),
            pltpu.VMEM(held, jnp.bfloat16),
            dma((chunks, GROUP - 1)), dma((chunks, GROUP - 1)),
            dma((GROUP - 1,)), dma((GROUP - 1,)),
            dma((3, chunks, 2)), dma((3, chunks, 2)),
            dma((chunks, others)), dma((chunks, others)),
            dma((2 * chunks + 2,)),
        ],
        compiler_params=pltpu.CompilerParams(
            collective_id=0, has_side_effects=True, vmem_limit_bytes=56 * 2**20
        ),
        name="filter_and_gram",
    )(orbitals, potential, band_matrix(8, ny), band_matrix(1, nz))


def rotate_kernel(own_ref, *refs):
    pieces, (first_ref, out_ref, wide) = refs[:-3], refs[-3:]
    count, rows, chunk, nz = pieces[0].shape
    orbs, all_rows = out_ref.shape[0], out_ref.shape[1]
    for j, piece in enumerate(pieces):
        start = first_ref[j]

        def body(i, _, piece=piece, start=start):
            x = jnp.concatenate(
                [piece[:, 2 * i + h].reshape(count * chunk, nz) for h in range(2)], axis=1
            )
            y = jnp.dot(own_ref[...], x, preferred_element_type=jnp.float32)
            for h in range(2):
                at = pl.ds(start + 2 * i + h, orbs, stride=all_rows)
                wide[at, :] = y[:, h * nz : (h + 1) * nz]
            return 0

        lax.fori_loop(0, rows // 2, body, 0)

    def narrow(i, _):
        part = wide[pl.ds(pl.multiple_of(i * 8 * all_rows, 8 * all_rows), 8 * all_rows), :]
        out_ref[pl.ds(i * 8, 8)] = part.reshape(8, all_rows, nz).astype(jnp.bfloat16)
        return 0

    lax.fori_loop(0, orbs // 8, narrow, 0)


def rotate(own_rows, pieces, firsts, all_rows):
    orbs = own_rows.shape[0]
    nz = pieces[0].shape[3]
    vmem = pl.BlockSpec(memory_space=pltpu.VMEM)
    return pl.pallas_call(
        rotate_kernel,
        out_shape=jax.ShapeDtypeStruct((orbs, all_rows, nz), jnp.bfloat16),
        in_specs=[vmem] * (1 + len(pieces)) + [pl.BlockSpec(memory_space=pltpu.SMEM)],
        out_specs=vmem,
        scratch_shapes=[pltpu.VMEM((orbs * all_rows, nz), jnp.float32)],
        compiler_params=pltpu.CompilerParams(vmem_limit_bytes=48 * 2**20),
        name="rotate",
    )(own_rows, *pieces, firsts)


def sum_kernel(bands, doms, scale, part_ref, out_ref, near, far, whole, *sems):
    near_send, near_recv, far_send, far_recv, all_send, all_recv = sems
    size = part_ref.shape[0]
    members = GROUP * bands
    rows = size // members
    z_count = doms // GROUP
    b, d = lax.axis_index("band"), lax.axis_index("dom")
    g, z = lax.rem(d, GROUP), d // GROUP
    others = [(k, j) for k in range(GROUP) for j in range(bands) if k or j]

    def place(k, j):
        return lax.rem(g + k, GROUP), lax.rem(b + j, bands)

    def near_device(k, j):
        to_g, to_b = place(k, j)
        return (to_b, z * GROUP + to_g)

    def far_device(h):
        return (b, lax.rem(z + h, z_count) * GROUP + g)

    def block(to_g, to_b):
        return pl.ds(pl.multiple_of((to_g * bands + to_b) * rows, rows), rows)

    barrier = pltpu.get_barrier_semaphore()
    for k, j in others:
        pl.semaphore_signal(barrier, inc=1, device_id=near_device(k, j), device_id_type=MESH)
    for h in range(1, z_count):
        pl.semaphore_signal(barrier, inc=1, device_id=far_device(h), device_id_type=MESH)
    pl.semaphore_wait(barrier, members - 1 + z_count - 1)

    copies = []
    for at, (k, j) in enumerate(others):
        copy = pltpu.make_async_remote_copy(
            part_ref.at[block(*place(k, j))], near.at[at], near_send.at[at], near_recv.at[at],
            device_id=near_device(k, j), device_id_type=MESH,
        )
        copy.start()
        copies.append(copy)
    total = part_ref[block(g, b), :]
    for at, copy in enumerate(copies):
        copy.wait_recv()
        total = total + near[at]
    far[z] = total
    for h in range(1, z_count):
        copy = pltpu.make_async_remote_copy(
            far.at[z], far.at[z], far_send.at[h - 1], far_recv.at[h - 1],
            device_id=far_device(h), device_id_type=MESH,
        )
        copy.start()
        copies.append(copy)
    for copy in copies[len(others):]:
        copy.wait_recv()
    total = far[0]
    for h in range(1, z_count):
        total = total + far[h]
    own = block(g, b)
    whole[own, :] = total * scale
    last = []
    for at, (k, j) in enumerate(others):
        copy = pltpu.make_async_remote_copy(
            whole.at[own], whole.at[own], all_send.at[at], all_recv.at[at],
            device_id=near_device(k, j), device_id_type=MESH,
        )
        copy.start()
        last.append(copy)
    for copy in last:
        copy.wait_recv()
    out_ref[...] = whole[...]
    for copy in copies + last:
        copy.wait_send()


def sum_everywhere(part, bands, doms, scale):
    size = part.shape[0]
    others = GROUP * bands - 1
    z_count = doms // GROUP
    rows = size // (GROUP * bands)
    dma = pltpu.SemaphoreType.DMA
    vmem = pl.BlockSpec(memory_space=pltpu.VMEM)
    far = max(z_count - 1, 1)
    return pl.pallas_call(
        functools.partial(sum_kernel, bands, doms, scale),
        out_shape=jax.ShapeDtypeStruct(part.shape, jnp.float32),
        in_specs=[vmem],
        out_specs=vmem,
        scratch_shapes=[
            pltpu.VMEM((others, rows, size), jnp.float32),
            pltpu.VMEM((z_count, rows, size), jnp.float32),
            pltpu.VMEM(part.shape, jnp.float32),
            dma((others,)), dma((others,)), dma((far,)), dma((far,)), dma((others,)), dma((others,)),
        ],
        compiler_params=pltpu.CompilerParams(
            collective_id=1, has_side_effects=True, vmem_limit_bytes=16 * 2**20
        ),
        name="sum_everywhere",
    )(part)


BLOCK = 128


def inverse_factor_kernel(gram_ref, out_ref, full, diag):
    size = gram_ref.shape[0]
    exact = lax.Precision.HIGHEST
    full[...] = gram_ref[...]
    row_id = lax.broadcasted_iota(jnp.int32, (BLOCK, BLOCK), 0)
    lane_id = lax.broadcasted_iota(jnp.int32, (BLOCK, BLOCK), 1)
    one_row = lax.broadcasted_iota(jnp.int32, (1, BLOCK), 1)
    for first in range(0, size, BLOCK):
        here, after = slice(first, first + BLOCK), first + BLOCK
        diag[...] = full[here, here]

        def eliminate(j, _):
            held = diag[...]
            row = diag[pl.ds(j, 1), :]
            pivot = jnp.sum(jnp.where(one_row == j, row, 0.0), axis=1, keepdims=True)
            column = jnp.sum(jnp.where(lane_id == j, held, 0.0), axis=1, keepdims=True)
            root = lax.rsqrt(pivot)
            root = root * (1.5 - 0.5 * pivot * root * root)
            scaled = jnp.where(one_row == j, 1.0, row) * root
            rest = jnp.where(lane_id == j, 0.0, held) - (column * root) * scaled
            diag[...] = jnp.where(row_id > j, rest, held)
            diag[pl.ds(j, 1), :] = scaled
            return 0

        lax.fori_loop(0, BLOCK, eliminate, 0)
        inverse = jnp.where(row_id >= lane_id, diag[...], 0.0)
        if first:
            full[here, :first] = jnp.dot(
                inverse, full[here, :first], precision=exact, preferred_element_type=jnp.float32
            )
        full[here, here] = inverse
        if after < size:
            upper = jnp.dot(
                inverse, full[here, after:], precision=exact, preferred_element_type=jnp.float32
            )
            full[here, after:] = upper
            full[after:, here] = jnp.zeros((size - after, BLOCK), jnp.float32)
            full[after:, :] -= lax.dot_general(
                upper, full[here, :], (((0,), (0,)), ((), ())),
                precision=exact, preferred_element_type=jnp.float32,
            )
    row_all = lax.broadcasted_iota(jnp.int32, (size, size), 0)
    lane_all = lax.broadcasted_iota(jnp.int32, (size, size), 1)
    out_ref[...] = jnp.where(row_all >= lane_all, full[...], 0.0).astype(jnp.bfloat16)


def rotation_from(gram):
    size = gram.shape[0]
    vmem = pl.BlockSpec(memory_space=pltpu.VMEM)
    return pl.pallas_call(
        inverse_factor_kernel,
        out_shape=jax.ShapeDtypeStruct(gram.shape, jnp.bfloat16),
        in_specs=[vmem],
        out_specs=vmem,
        scratch_shapes=[
            pltpu.VMEM(gram.shape, jnp.float32), pltpu.VMEM((BLOCK, BLOCK), jnp.float32)
        ],
        compiler_params=pltpu.CompilerParams(vmem_limit_bytes=16 * 2**20),
        cost_estimate=pl.CostEstimate(
            flops=40 * size**3, bytes_accessed=100 * 2**20, transcendentals=0
        ),
        name="inverse_factor",
    )(gram)


def local(bands, doms, orbitals, potential):
    orbs, planes, ny, nz = orbitals.shape
    all_rows = planes * ny
    total_cells = all_rows * nz * doms
    part, held = filter_and_gram(orbitals, potential, bands, doms)
    pieces = [held]
    for j in range(1, bands):
        ring = [((i + j) % bands, i) for i in range(bands)]
        pieces.append(lax.ppermute(held, "band", ring))
    gram = sum_everywhere(part, bands, doms, 1.0 / total_cells)
    rotation = rotation_from(gram)
    b = lax.axis_index("band")
    own_rows = lax.dynamic_slice_in_dim(rotation, b * orbs, orbs, 0)
    firsts = (b + jnp.arange(bands, dtype=jnp.int32)) % bands * (all_rows // bands)
    result = rotate(own_rows, pieces, firsts.astype(jnp.int32), all_rows)
    return result.reshape(orbitals.shape)


def solution(mesh):
    placed = (P("band", "dom", None, None), P("dom", None, None))
    return jax.shard_map(
        functools.partial(local, mesh.shape["band"], mesh.shape["dom"]),
        mesh=mesh, in_specs=placed, out_specs=P("band", "dom", None, None), check_vma=False,
    )
```

```python
import functools

import jax
import jax.numpy as jnp
import numpy as np
from jax import lax
from jax.experimental import pallas as pl
from jax.experimental.pallas import tpu as pltpu
from jax.sharding import PartitionSpec as P

MESH = pl.DeviceIdType.MESH
spectrum_center = 7.5
spectrum_half = 4.5
GROUP = 4
CHUNK = 16


def band_matrix(blocks, size):
    one = 16.0 * (np.eye(size, k=1) + np.eye(size, k=-1)) - np.eye(size, k=2) - np.eye(size, k=-2)
    return jnp.asarray(np.kron(np.eye(blocks), one), jnp.bfloat16)


def filter_kernel(
    bands, doms, orb_ref, pot_ref, ty_ref, tz_ref, gram_ref, held_ref, kept_ref,
    f0, f1, f2, pot, wide, sent, held,
    in_send, in_recv, pot_send, pot_recv, halo_send, halo_recv, out_send, out_recv, own_sem,
):
    orbs, planes, ny, nz = orb_ref.shape
    share = orbs // GROUP
    slab = GROUP * planes
    chunks = share // CHUNK
    rows_dev = planes * ny
    rows_part = rows_dev // bands
    b, d = lax.axis_index("band"), lax.axis_index("dom")
    g, z = lax.rem(d, GROUP), d // GROUP
    z_count = doms // GROUP
    base = z * GROUP
    has_low, has_high = z > 0, z < z_count - 1

    def peer(k, j=0):
        return (lax.rem(b + j, bands), base + lax.rem(g + k, GROUP))

    barrier = pltpu.get_barrier_semaphore()
    for k in range(GROUP):
        for j in range(bands):
            if k or j:
                pl.semaphore_signal(barrier, inc=1, device_id=peer(k, j), device_id_type=MESH)

    @pl.when(has_low)
    def _():
        pl.semaphore_signal(barrier, inc=1, device_id=(b, d - GROUP), device_id_type=MESH)

    @pl.when(has_high)
    def _():
        pl.semaphore_signal(barrier, inc=1, device_id=(b, d + GROUP), device_id_type=MESH)

    ends = jnp.where(has_low, 1, 0) + jnp.where(has_high, 1, 0)
    pl.semaphore_wait(barrier, GROUP * bands - 1 + ends)

    pot_copies, in_copies = [], {}
    own_planes = pl.ds(g * planes, planes)
    for k in range(1, GROUP):
        copy = pltpu.make_async_remote_copy(
            pot_ref, pot.at[own_planes], pot_send.at[k - 1], pot_recv.at[k - 1],
            device_id=peer(k), device_id_type=MESH,
        )
        copy.start()
        pot_copies.append(copy)
    own_pot = pltpu.make_async_copy(pot_ref, pot.at[own_planes], own_sem.at[chunks])
    own_pot.start()
    own_in = []
    for c in range(chunks):
        span = pl.ds(c * CHUNK, CHUNK)
        landing = f0.at[span, pl.ds(2 + g * planes, planes)]
        for k in range(1, GROUP):
            first = lax.rem(g + k, GROUP) * share + c * CHUNK
            copy = pltpu.make_async_remote_copy(
                orb_ref.at[pl.ds(first, CHUNK)], landing,
                in_send.at[c, k - 1], in_recv.at[c, k - 1],
                device_id=peer(k), device_id_type=MESH,
            )
            copy.start()
            in_copies[c, k] = copy
        copy = pltpu.make_async_copy(
            orb_ref.at[pl.ds(g * share + c * CHUNK, CHUNK)], landing, own_sem.at[c]
        )
        copy.start()
        own_in.append(copy)

    fields = (f0, f1, f2)

    @pl.when(jnp.logical_not(has_low))
    def _():
        for field in fields:
            field[:, 0:2] = jnp.zeros((share, 2, ny, nz), jnp.bfloat16)

    @pl.when(jnp.logical_not(has_high))
    def _():
        for field in fields:
            field[:, slab + 2 :] = jnp.zeros((share, 2, ny, nz), jnp.bfloat16)

    def halo(s, c):
        field, span = fields[s], pl.ds(c * CHUNK, CHUNK)
        down = pltpu.make_async_remote_copy(
            field.at[span, pl.ds(2, 2)], field.at[span, pl.ds(slab + 2, 2)],
            halo_send.at[s, c, 0], halo_recv.at[s, c, 0],
            device_id=(b, d - GROUP), device_id_type=MESH,
        )
        up = pltpu.make_async_remote_copy(
            field.at[span, pl.ds(slab, 2)], field.at[span, pl.ds(0, 2)],
            halo_send.at[s, c, 1], halo_recv.at[s, c, 1],
            device_id=(b, d + GROUP), device_id_type=MESH,
        )
        return down, up

    def send_halo(s, c):
        down, up = halo(s, c)
        pl.when(has_low)(down.start)
        pl.when(has_high)(up.start)

    def wait_halo(s, c):
        down, up = halo(s, c)
        pl.when(has_low)(up.wait_recv)
        pl.when(has_high)(down.wait_recv)

    def wait_halo_sent(s, c):
        down, up = halo(s, c)
        pl.when(has_low)(down.wait_send)
        pl.when(has_high)(up.wait_send)

    def apply(s, c):
        field = fields[s]
        factor = (1.0 if s == 0 else 2.0) / spectrum_half
        shift = 0.5 * 7.5 - spectrum_center

        def value(p, first):
            span = pl.ds(first, 8)

            def at(q):
                return field[span, q].reshape(8 * ny, nz)

            def wide_at(q):
                return at(q).astype(jnp.float32)

            v = at(p + 2)
            total = jnp.dot(ty_ref[...], v, preferred_element_type=jnp.float32)
            total += jnp.dot(v, tz_ref[...], preferred_element_type=jnp.float32)
            total += 16.0 * (wide_at(p + 1) + wide_at(p + 3)) - (wide_at(p) + wide_at(p + 4))
            scale = (pot[p] + shift) * factor
            own = (v.astype(jnp.float32).reshape(8, ny, nz) * scale[None]).reshape(8 * ny, nz)
            new = own - total * (factor / 24.0)
            if s > 0:
                old = fields[s - 1][span, p + 2].reshape(8 * ny, nz)
                new = new - old.astype(jnp.float32)
            return new

        if s < 2:
            def body(i, _):
                p, first = i // 2, pl.multiple_of(c * CHUNK + lax.rem(i, 2) * 8, 8)
                new = value(p, first).astype(jnp.bfloat16)
                fields[s + 1][pl.ds(first, 8), p + 2] = new.reshape(8, ny, nz)
                return 0

            lax.fori_loop(0, 2 * slab, body, 0)
        else:
            def body(p, _):
                for h in range(2):
                    wide[pl.ds(h * 8 * ny, 8 * ny), :] = value(p, c * CHUNK + h * 8)
                for y in range(ny):
                    rows = wide[pl.ds(y, CHUNK, stride=ny), :]
                    sent[c, p * ny + y] = rows.astype(jnp.bfloat16)
                return 0

            lax.fori_loop(0, slab, body, 0)

    own_out, out_copies, kept = [], [], []

    def send_out(c):
        landing = held.at[(b * GROUP + g) * chunks + c]
        copy = pltpu.make_async_copy(sent.at[c], kept_ref.at[c], own_sem.at[2 * chunks + 2 + c])
        copy.start()
        kept.append(copy)
        for k in range(GROUP):
            for j in range(bands):
                row = lax.rem(g + k, GROUP) * rows_dev + lax.rem(b + j, bands) * rows_part
                source = sent.at[c, pl.ds(row, rows_part)]
                if k or j:
                    at = k * bands + j - 1
                    copy = pltpu.make_async_remote_copy(
                        source, landing, out_send.at[c, at], out_recv.at[c, at],
                        device_id=peer(k, j), device_id_type=MESH,
                    )
                    out_copies.append(copy)
                else:
                    copy = pltpu.make_async_copy(source, landing, own_sem.at[chunks + 1 + c])
                    own_out.append(copy)
                copy.start()

    for copy in pot_copies:
        copy.wait_recv()
    own_pot.wait()
    for t in range(chunks + 3):
        if t < chunks:
            own_in[t].wait()
            for k in range(1, GROUP):
                in_copies[t, k].wait_recv()
            send_halo(0, t)
        for s in (2, 1, 0):
            c = t - 1 - s
            if 0 <= c < chunks:
                wait_halo(s, c)
                apply(s, c)
                if s < 2:
                    send_halo(s + 1, c)
                else:
                    send_out(c)

    for copy in own_out:
        copy.wait()
    for copy in out_copies:
        copy.wait_recv()
    keep = pltpu.make_async_copy(held, held_ref, own_sem.at[2 * chunks + 1])
    keep.start()

    everyone = bands * orbs
    step = min(8, rows_part)

    def terms(i, _):
        x = jnp.concatenate(
            [held[:, i * step + j].reshape(everyone, nz) for j in range(step)], axis=1
        )
        part = lax.dot_general(
            x, x, (((1,), (1,)), ((), ())), preferred_element_type=jnp.float32
        )
        gram_ref[...] += part
        return 0

    gram_ref[...] = jnp.zeros(gram_ref.shape, jnp.float32)
    lax.fori_loop(0, rows_part // step, terms, 0)

    for copy in pot_copies:
        copy.wait_send()
    for copy in in_copies.values():
        copy.wait_send()
    for s in range(3):
        for c in range(chunks):
            wait_halo_sent(s, c)
    for copy in out_copies:
        copy.wait_send()
    for copy in kept:
        copy.wait()
    keep.wait()


def filter_and_gram(orbitals, potential, bands, doms):
    orbs, planes, ny, nz = orbitals.shape
    share, slab = orbs // GROUP, GROUP * planes
    chunks = share // CHUNK
    rows_part = planes * ny // bands
    held = (bands * orbs // CHUNK, rows_part, CHUNK, nz)
    field = pltpu.VMEM((share, slab + 4, ny, nz), jnp.bfloat16)
    others = GROUP * bands - 1
    dma = pltpu.SemaphoreType.DMA
    vmem = pl.BlockSpec(memory_space=pltpu.VMEM)
    hbm = pl.BlockSpec(memory_space=pl.ANY)
    return pl.pallas_call(
        functools.partial(filter_kernel, bands, doms),
        out_shape=(
            jax.ShapeDtypeStruct((bands * orbs, bands * orbs), jnp.float32),
            jax.ShapeDtypeStruct(held, jnp.bfloat16),
            jax.ShapeDtypeStruct((chunks, slab * ny, CHUNK, nz), jnp.bfloat16),
        ),
        in_specs=[hbm, vmem, vmem, vmem],
        out_specs=(vmem, hbm, hbm),
        scratch_shapes=[
            field, field, field,
            pltpu.VMEM((slab, ny, nz), jnp.float32),
            pltpu.VMEM((CHUNK * ny, nz), jnp.float32),
            pltpu.VMEM((chunks, slab * ny, CHUNK, nz), jnp.bfloat16),
            pltpu.VMEM(held, jnp.bfloat16),
            dma((chunks, GROUP - 1)), dma((chunks, GROUP - 1)),
            dma((GROUP - 1,)), dma((GROUP - 1,)),
            dma((3, chunks, 2)), dma((3, chunks, 2)),
            dma((chunks, others)), dma((chunks, others)),
            dma((3 * chunks + 2,)),
        ],
        compiler_params=pltpu.CompilerParams(
            collective_id=0, has_side_effects=True, vmem_limit_bytes=56 * 2**20
        ),
        name="filter_and_gram",
    )(orbitals, potential, band_matrix(8, ny), band_matrix(1, nz))


def rotate_kernel(counts, first_ref, *refs):
    refs, (out_ref, wide) = refs[:-2], refs[-2:]
    orbs, all_rows = out_ref.shape[0], out_ref.shape[1]
    taken = 0
    for at, count in enumerate(counts):
        weight, parts = refs[taken], refs[taken + 1 : taken + 1 + count]
        taken += 1 + count
        rows, chunk, nz = parts[0].shape[1:]
        start = first_ref[at]

        def body(i, _, weight=weight, parts=parts, start=start, chunk=chunk, nz=nz):
            def orbitals_at(row):
                return jnp.concatenate(
                    [part[:, row].reshape(part.shape[0] * chunk, nz) for part in parts], axis=0
                )

            x = jnp.concatenate([orbitals_at(2 * i), orbitals_at(2 * i + 1)], axis=1)
            y = jnp.dot(weight[...], x, preferred_element_type=jnp.float32)
            for h in range(2):
                wide[pl.ds(start + 2 * i + h, orbs, stride=all_rows), :] = y[:, h * nz : (h + 1) * nz]
            return 0

        lax.fori_loop(0, rows // 2, body, 0)

    def narrow(i, _):
        part = wide[pl.ds(pl.multiple_of(i * 8 * all_rows, 8 * all_rows), 8 * all_rows), :]
        out_ref[pl.ds(i * 8, 8)] = part.reshape(8, all_rows, -1).astype(jnp.bfloat16)
        return 0

    lax.fori_loop(0, orbs // 8, narrow, 0)


def rotate(pieces, firsts, all_rows):
    orbs = pieces[0][0].shape[0]
    nz = pieces[0][1].shape[3]
    vmem = pl.BlockSpec(memory_space=pltpu.VMEM)
    operands = [array for piece in pieces for array in piece]
    return pl.pallas_call(
        functools.partial(rotate_kernel, [len(piece) - 1 for piece in pieces]),
        out_shape=jax.ShapeDtypeStruct((orbs, all_rows, nz), jnp.bfloat16),
        in_specs=[pl.BlockSpec(memory_space=pltpu.SMEM)] + [vmem] * len(operands),
        out_specs=vmem,
        scratch_shapes=[pltpu.VMEM((orbs * all_rows, nz), jnp.float32)],
        compiler_params=pltpu.CompilerParams(vmem_limit_bytes=48 * 2**20),
        name="rotate",
    )(firsts, *operands)


def sum_kernel(bands, doms, scale, part_ref, out_ref, near, far, whole, *sems):
    near_send, near_recv, far_send, far_recv, all_send, all_recv = sems
    size = part_ref.shape[0]
    members = GROUP * bands
    rows = size // members
    z_count = doms // GROUP
    b, d = lax.axis_index("band"), lax.axis_index("dom")
    g, z = lax.rem(d, GROUP), d // GROUP
    others = [(k, j) for k in range(GROUP) for j in range(bands) if k or j]

    def place(k, j):
        return lax.rem(g + k, GROUP), lax.rem(b + j, bands)

    def near_device(k, j):
        to_g, to_b = place(k, j)
        return (to_b, z * GROUP + to_g)

    def far_device(h):
        return (b, lax.rem(z + h, z_count) * GROUP + g)

    def block(to_g, to_b):
        return pl.ds(pl.multiple_of((to_g * bands + to_b) * rows, rows), rows)

    barrier = pltpu.get_barrier_semaphore()
    for k, j in others:
        pl.semaphore_signal(barrier, inc=1, device_id=near_device(k, j), device_id_type=MESH)
    for h in range(1, z_count):
        pl.semaphore_signal(barrier, inc=1, device_id=far_device(h), device_id_type=MESH)
    pl.semaphore_wait(barrier, members - 1 + z_count - 1)

    copies = []
    for at, (k, j) in enumerate(others):
        copy = pltpu.make_async_remote_copy(
            part_ref.at[block(*place(k, j))], near.at[at], near_send.at[at], near_recv.at[at],
            device_id=near_device(k, j), device_id_type=MESH,
        )
        copy.start()
        copies.append(copy)
    total = part_ref[block(g, b), :]
    for at, copy in enumerate(copies):
        copy.wait_recv()
        total = total + near[at]
    far[z] = total
    for h in range(1, z_count):
        copy = pltpu.make_async_remote_copy(
            far.at[z], far.at[z], far_send.at[h - 1], far_recv.at[h - 1],
            device_id=far_device(h), device_id_type=MESH,
        )
        copy.start()
        copies.append(copy)
    for copy in copies[len(others):]:
        copy.wait_recv()
    total = far[0]
    for h in range(1, z_count):
        total = total + far[h]
    own = block(g, b)
    whole[own, :] = total * scale
    last = []
    for at, (k, j) in enumerate(others):
        copy = pltpu.make_async_remote_copy(
            whole.at[own], whole.at[own], all_send.at[at], all_recv.at[at],
            device_id=near_device(k, j), device_id_type=MESH,
        )
        copy.start()
        last.append(copy)
    for copy in last:
        copy.wait_recv()
    out_ref[...] = whole[...]
    for copy in copies + last:
        copy.wait_send()


def sum_everywhere(part, bands, doms, scale):
    size = part.shape[0]
    others = GROUP * bands - 1
    z_count = doms // GROUP
    rows = size // (GROUP * bands)
    dma = pltpu.SemaphoreType.DMA
    vmem = pl.BlockSpec(memory_space=pltpu.VMEM)
    far = max(z_count - 1, 1)
    return pl.pallas_call(
        functools.partial(sum_kernel, bands, doms, scale),
        out_shape=jax.ShapeDtypeStruct(part.shape, jnp.float32),
        in_specs=[vmem],
        out_specs=vmem,
        scratch_shapes=[
            pltpu.VMEM((others, rows, size), jnp.float32),
            pltpu.VMEM((z_count, rows, size), jnp.float32),
            pltpu.VMEM(part.shape, jnp.float32),
            dma((others,)), dma((others,)), dma((far,)), dma((far,)), dma((others,)), dma((others,)),
        ],
        compiler_params=pltpu.CompilerParams(
            collective_id=1, has_side_effects=True, vmem_limit_bytes=16 * 2**20
        ),
        name="sum_everywhere",
    )(part)


BLOCK = 128
PIVOTS = 4


def eliminate(diag, low, i, _):
    first = low + i * PIVOTS
    held = diag[low:, :]
    row_id = lax.broadcasted_iota(jnp.int32, held.shape, 0) + low
    lane_id = lax.broadcasted_iota(jnp.int32, held.shape, 1)
    one_row = lax.broadcasted_iota(jnp.int32, (1, BLOCK), 1)
    rows = [diag[pl.ds(first + p, 1), :] for p in range(PIVOTS)]

    def pick(p, q):
        return jnp.sum(jnp.where(one_row == first + q, rows[p], 0.0), axis=1, keepdims=True)

    corner = [[pick(p, q) if q >= p else None for q in range(PIVOTS)] for p in range(PIVOTS)]
    columns = [
        jnp.sum(jnp.where(lane_id == first + p, held, 0.0), axis=1, keepdims=True)
        for p in range(PIVOTS)
    ]
    roots, lower = [], [[None] * PIVOTS for _ in range(PIVOTS)]
    for p in range(PIVOTS):
        pivot = corner[p][p]
        root = lax.rsqrt(pivot)
        root = root * (1.5 - 0.5 * pivot * root * root)
        roots.append(root)
        for q in range(p + 1, PIVOTS):
            lower[q][p] = corner[p][q] * root
        for q in range(p + 1, PIVOTS):
            for t in range(q, PIVOTS):
                corner[q][t] = corner[q][t] - lower[q][p] * lower[t][p]
    inside = (one_row >= first) & (one_row < first + PIVOTS)
    rest = jnp.where((lane_id >= first) & (lane_id < first + PIVOTS), 0.0, held)
    scaled, factors = [], []
    for p in range(PIVOTS):
        row = jnp.where(one_row == first + p, 1.0, jnp.where(inside, 0.0, rows[p]))
        column = columns[p]
        for t in range(p):
            row = row - lower[p][t] * scaled[t]
            column = column - factors[t] * lower[p][t]
        scaled.append(row * roots[p])
        factors.append(column * roots[p])
        rest = rest - factors[p] * scaled[p]
    diag[low:, :] = jnp.where(row_id >= first + PIVOTS, rest, held)
    for p in range(PIVOTS):
        diag[pl.ds(first + p, 1), :] = scaled[p]
    return 0


def inverse_factor_kernel(gram_ref, out_ref, full, diag):
    size = gram_ref.shape[0]
    exact = lax.Precision.HIGHEST
    full[...] = gram_ref[...]
    row_id = lax.broadcasted_iota(jnp.int32, (BLOCK, BLOCK), 0)
    lane_id = lax.broadcasted_iota(jnp.int32, (BLOCK, BLOCK), 1)
    for first in range(0, size, BLOCK):
        here, after = slice(first, first + BLOCK), first + BLOCK
        diag[...] = full[here, here]

        for low in range(0, BLOCK, BLOCK // 4):
            eliminate_from = functools.partial(eliminate, diag, low)
            lax.fori_loop(0, BLOCK // 4 // PIVOTS, eliminate_from, 0)
        inverse = jnp.where(row_id >= lane_id, diag[...], 0.0)
        if first:
            full[here, :first] = jnp.dot(
                inverse, full[here, :first], precision=exact, preferred_element_type=jnp.float32
            )
        full[here, here] = inverse
        if after < size:
            upper = jnp.dot(
                inverse, full[here, after:], precision=exact, preferred_element_type=jnp.float32
            )
            full[here, after:] = upper
            full[after:, here] = jnp.zeros((size - after, BLOCK), jnp.float32)
            full[after:, :] -= lax.dot_general(
                upper, full[here, :], (((0,), (0,)), ((), ())),
                precision=exact, preferred_element_type=jnp.float32,
            )
    row_all = lax.broadcasted_iota(jnp.int32, (size, size), 0)
    lane_all = lax.broadcasted_iota(jnp.int32, (size, size), 1)
    out_ref[...] = jnp.where(row_all >= lane_all, full[...], 0.0).astype(jnp.bfloat16)


def rotation_from(gram):
    size = gram.shape[0]
    vmem = pl.BlockSpec(memory_space=pltpu.VMEM)
    return pl.pallas_call(
        inverse_factor_kernel,
        out_shape=jax.ShapeDtypeStruct(gram.shape, jnp.bfloat16),
        in_specs=[vmem],
        out_specs=vmem,
        scratch_shapes=[
            pltpu.VMEM(gram.shape, jnp.float32), pltpu.VMEM((BLOCK, BLOCK), jnp.float32)
        ],
        compiler_params=pltpu.CompilerParams(vmem_limit_bytes=16 * 2**20),
        cost_estimate=pl.CostEstimate(
            flops=40 * size**3, bytes_accessed=100 * 2**20, transcendentals=0
        ),
        name="inverse_factor",
    )(gram)


def local(bands, doms, orbitals, potential):
    orbs, planes, ny, nz = orbitals.shape
    all_rows = planes * ny
    total_cells = all_rows * nz * doms
    part, held, kept = filter_and_gram(orbitals, potential, bands, doms)
    gram = sum_everywhere(part, bands, doms, 1.0 / total_cells)
    gram, held, kept = lax.optimization_barrier((gram, held, kept))
    b, d = lax.axis_index("band"), lax.axis_index("dom")
    rows_part = all_rows // bands
    if bands == 2:
        g = d % GROUP
        share = orbs // GROUP
        count = orbs // CHUNK
        partner = lax.dynamic_slice_in_dim(held, b * count, count, 0)
        partner = lax.ppermute(partner, "band", [(0, 1), (1, 0)])
        near = []
        for k in range(GROUP):
            row = (g + k) % GROUP * all_rows + (1 - b) * rows_part
            piece = lax.dynamic_slice_in_dim(kept, row, rows_part, 1)
            if k:
                ring = [(i, i // GROUP * GROUP + (i + k) % GROUP) for i in range(doms)]
                piece = lax.ppermute(piece, "dom", ring)
            near.append(piece)
    else:
        rings = [[((i + j) % bands, i) for i in range(bands)] for j in range(1, bands)]
        others = [lax.ppermute(held, "band", ring) for ring in rings]
    rotation = rotation_from(gram)
    own_rows = lax.dynamic_slice_in_dim(rotation, b * orbs, orbs, 0)
    pieces = [[own_rows, held]]
    if bands == 2:
        starts = [b * orbs + (g - k) % GROUP * share for k in range(GROUP)]
        columns = [lax.dynamic_slice_in_dim(own_rows, start, share, 1) for start in starts]
        columns.append(lax.dynamic_slice_in_dim(own_rows, (1 - b) * orbs, orbs, 1))
        pieces.append([jnp.concatenate(columns, axis=1), *near, partner])
    else:
        pieces += [[own_rows, other] for other in others]
    firsts = (b + jnp.arange(bands, dtype=jnp.int32)) % bands * rows_part
    result = rotate(pieces, firsts.astype(jnp.int32), all_rows)
    return result.reshape(orbitals.shape)


def solution(mesh):
    placed = (P("band", "dom", None, None), P("dom", None, None))
    return jax.shard_map(
        functools.partial(local, mesh.shape["band"], mesh.shape["dom"]),
        mesh=mesh, in_specs=placed, out_specs=P("band", "dom", None, None), check_vma=False,
    )
```

```python
import functools

import jax
import jax.numpy as jnp
import numpy as np
from jax import lax
from jax.experimental import pallas as pl
from jax.experimental.pallas import tpu as pltpu
from jax.sharding import PartitionSpec as P

MESH = pl.DeviceIdType.MESH
spectrum_center = 7.5
spectrum_half = 4.5
GROUP = 4
CHUNK = 16


def band_matrix(blocks, size):
    one = 16.0 * (np.eye(size, k=1) + np.eye(size, k=-1)) - np.eye(size, k=2) - np.eye(size, k=-2)
    return jnp.asarray(np.kron(np.eye(blocks), one), jnp.bfloat16)


BLOCK = 128


def lower_blocks(size):
    count = size // BLOCK
    return [(i, j) for i in range(count) for j in range(i + 1)]


def filter_kernel(
    bands, doms, orb_ref, pot_ref, ty_ref, tz_ref, gram_ref, held_ref, kept_ref,
    f0, f1, f2, pot, wide, sent, held,
    in_send, in_recv, pot_send, pot_recv, halo_send, halo_recv, out_send, out_recv, own_sem,
):
    orbs, planes, ny, nz = orb_ref.shape
    share = orbs // GROUP
    slab = GROUP * planes
    chunks = share // CHUNK
    rows_dev = planes * ny
    rows_part = rows_dev // bands
    b, d = lax.axis_index("band"), lax.axis_index("dom")
    g, z = lax.rem(d, GROUP), d // GROUP
    z_count = doms // GROUP
    base = z * GROUP
    has_low, has_high = z > 0, z < z_count - 1

    def peer(k, j=0):
        return (lax.rem(b + j, bands), base + lax.rem(g + k, GROUP))

    barrier = pltpu.get_barrier_semaphore()
    for k in range(GROUP):
        for j in range(bands):
            if k or j:
                pl.semaphore_signal(barrier, inc=1, device_id=peer(k, j), device_id_type=MESH)

    @pl.when(has_low)
    def _():
        pl.semaphore_signal(barrier, inc=1, device_id=(b, d - GROUP), device_id_type=MESH)

    @pl.when(has_high)
    def _():
        pl.semaphore_signal(barrier, inc=1, device_id=(b, d + GROUP), device_id_type=MESH)

    ends = jnp.where(has_low, 1, 0) + jnp.where(has_high, 1, 0)
    pl.semaphore_wait(barrier, GROUP * bands - 1 + ends)

    pot_copies, in_copies = [], {}
    own_planes = pl.ds(g * planes, planes)
    for k in range(1, GROUP):
        copy = pltpu.make_async_remote_copy(
            pot_ref, pot.at[own_planes], pot_send.at[k - 1], pot_recv.at[k - 1],
            device_id=peer(k), device_id_type=MESH,
        )
        copy.start()
        pot_copies.append(copy)
    own_pot = pltpu.make_async_copy(pot_ref, pot.at[own_planes], own_sem.at[chunks])
    own_pot.start()
    own_in = []
    for c in range(chunks):
        span = pl.ds(c * CHUNK, CHUNK)
        landing = f0.at[span, pl.ds(2 + g * planes, planes)]
        for k in range(1, GROUP):
            first = lax.rem(g + k, GROUP) * share + c * CHUNK
            copy = pltpu.make_async_remote_copy(
                orb_ref.at[pl.ds(first, CHUNK)], landing,
                in_send.at[c, k - 1], in_recv.at[c, k - 1],
                device_id=peer(k), device_id_type=MESH,
            )
            copy.start()
            in_copies[c, k] = copy
        copy = pltpu.make_async_copy(
            orb_ref.at[pl.ds(g * share + c * CHUNK, CHUNK)], landing, own_sem.at[c]
        )
        copy.start()
        own_in.append(copy)

    fields = (f0, f1, f2)

    @pl.when(jnp.logical_not(has_low))
    def _():
        for field in fields:
            field[:, 0:2] = jnp.zeros((share, 2, ny, nz), jnp.bfloat16)

    @pl.when(jnp.logical_not(has_high))
    def _():
        for field in fields:
            field[:, slab + 2 :] = jnp.zeros((share, 2, ny, nz), jnp.bfloat16)

    def halo(s, c):
        field, span = fields[s], pl.ds(c * CHUNK, CHUNK)
        down = pltpu.make_async_remote_copy(
            field.at[span, pl.ds(2, 2)], field.at[span, pl.ds(slab + 2, 2)],
            halo_send.at[s, c, 0], halo_recv.at[s, c, 0],
            device_id=(b, d - GROUP), device_id_type=MESH,
        )
        up = pltpu.make_async_remote_copy(
            field.at[span, pl.ds(slab, 2)], field.at[span, pl.ds(0, 2)],
            halo_send.at[s, c, 1], halo_recv.at[s, c, 1],
            device_id=(b, d + GROUP), device_id_type=MESH,
        )
        return down, up

    def send_halo(s, c):
        down, up = halo(s, c)
        pl.when(has_low)(down.start)
        pl.when(has_high)(up.start)

    def wait_halo(s, c):
        down, up = halo(s, c)
        pl.when(has_low)(up.wait_recv)
        pl.when(has_high)(down.wait_recv)

    def wait_halo_sent(s, c):
        down, up = halo(s, c)
        pl.when(has_low)(down.wait_send)
        pl.when(has_high)(up.wait_send)

    def apply(s, c):
        field = fields[s]
        factor = (1.0 if s == 0 else 2.0) / spectrum_half
        shift = 0.5 * 7.5 - spectrum_center

        def value(p, first):
            span = pl.ds(first, 8)

            def at(q):
                return field[span, q].reshape(8 * ny, nz)

            def wide_at(q):
                return at(q).astype(jnp.float32)

            v = at(p + 2)
            total = jnp.dot(ty_ref[...], v, preferred_element_type=jnp.float32)
            total += jnp.dot(v, tz_ref[...], preferred_element_type=jnp.float32)
            total += 16.0 * (wide_at(p + 1) + wide_at(p + 3)) - (wide_at(p) + wide_at(p + 4))
            scale = (pot[p] + shift) * factor
            own = (v.astype(jnp.float32).reshape(8, ny, nz) * scale[None]).reshape(8 * ny, nz)
            new = own - total * (factor / 24.0)
            if s > 0:
                old = fields[s - 1][span, p + 2].reshape(8 * ny, nz)
                new = new - old.astype(jnp.float32)
            return new

        if s < 2:
            def body(i, _):
                p, first = i // 2, pl.multiple_of(c * CHUNK + lax.rem(i, 2) * 8, 8)
                new = value(p, first).astype(jnp.bfloat16)
                fields[s + 1][pl.ds(first, 8), p + 2] = new.reshape(8, ny, nz)
                return 0

            lax.fori_loop(0, 2 * slab, body, 0)
        else:
            def body(p, _):
                for h in range(2):
                    wide[pl.ds(h * 8 * ny, 8 * ny), :] = value(p, c * CHUNK + h * 8)
                for y in range(ny):
                    rows = wide[pl.ds(y, CHUNK, stride=ny), :]
                    sent[c, p * ny + y] = rows.astype(jnp.bfloat16)
                return 0

            lax.fori_loop(0, slab, body, 0)

    own_out, out_copies, kept = [], [], []

    def send_out(c):
        landing = held.at[(b * GROUP + g) * chunks + c]
        copy = pltpu.make_async_copy(sent.at[c], kept_ref.at[c], own_sem.at[2 * chunks + 2 + c])
        copy.start()
        kept.append(copy)
        for k in range(GROUP):
            for j in range(bands):
                row = lax.rem(g + k, GROUP) * rows_dev + lax.rem(b + j, bands) * rows_part
                source = sent.at[c, pl.ds(row, rows_part)]
                if k or j:
                    at = k * bands + j - 1
                    copy = pltpu.make_async_remote_copy(
                        source, landing, out_send.at[c, at], out_recv.at[c, at],
                        device_id=peer(k, j), device_id_type=MESH,
                    )
                    out_copies.append(copy)
                else:
                    copy = pltpu.make_async_copy(source, landing, own_sem.at[chunks + 1 + c])
                    own_out.append(copy)
                copy.start()

    for copy in pot_copies:
        copy.wait_recv()
    own_pot.wait()
    for t in range(chunks + 3):
        if t < chunks:
            own_in[t].wait()
            for k in range(1, GROUP):
                in_copies[t, k].wait_recv()
            send_halo(0, t)
        for s in (2, 1, 0):
            c = t - 1 - s
            if 0 <= c < chunks:
                wait_halo(s, c)
                apply(s, c)
                if s < 2:
                    send_halo(s + 1, c)
                else:
                    send_out(c)

    for copy in own_out:
        copy.wait()
    for copy in out_copies:
        copy.wait_recv()
    keep = pltpu.make_async_copy(held, held_ref, own_sem.at[2 * chunks + 1])
    keep.start()

    everyone = bands * orbs
    step = min(8, rows_part)

    def terms(i, _):
        x = jnp.concatenate(
            [held[:, i * step + j].reshape(everyone, nz) for j in range(step)], axis=1
        )
        part = lax.dot_general(
            x, x, (((1,), (1,)), ((), ())), preferred_element_type=jnp.float32
        )
        for at, (i, j) in enumerate(lower_blocks(everyone)):
            tile = part[i * BLOCK : (i + 1) * BLOCK, j * BLOCK : (j + 1) * BLOCK]
            gram_ref[at * BLOCK : (at + 1) * BLOCK, :] += tile
        return 0

    gram_ref[...] = jnp.zeros(gram_ref.shape, jnp.float32)
    lax.fori_loop(0, rows_part // step, terms, 0)

    for copy in pot_copies:
        copy.wait_send()
    for copy in in_copies.values():
        copy.wait_send()
    for s in range(3):
        for c in range(chunks):
            wait_halo_sent(s, c)
    for copy in out_copies:
        copy.wait_send()
    for copy in kept:
        copy.wait()
    keep.wait()


def filter_and_gram(orbitals, potential, bands, doms):
    orbs, planes, ny, nz = orbitals.shape
    share, slab = orbs // GROUP, GROUP * planes
    chunks = share // CHUNK
    rows_part = planes * ny // bands
    held = (bands * orbs // CHUNK, rows_part, CHUNK, nz)
    field = pltpu.VMEM((share, slab + 4, ny, nz), jnp.bfloat16)
    others = GROUP * bands - 1
    dma = pltpu.SemaphoreType.DMA
    vmem = pl.BlockSpec(memory_space=pltpu.VMEM)
    hbm = pl.BlockSpec(memory_space=pl.ANY)
    return pl.pallas_call(
        functools.partial(filter_kernel, bands, doms),
        out_shape=(
            jax.ShapeDtypeStruct(
                (len(lower_blocks(bands * orbs)) * BLOCK, BLOCK), jnp.float32
            ),
            jax.ShapeDtypeStruct(held, jnp.bfloat16),
            jax.ShapeDtypeStruct((chunks, slab * ny, CHUNK, nz), jnp.bfloat16),
        ),
        in_specs=[hbm, vmem, vmem, vmem],
        out_specs=(vmem, hbm, hbm),
        scratch_shapes=[
            field, field, field,
            pltpu.VMEM((slab, ny, nz), jnp.float32),
            pltpu.VMEM((CHUNK * ny, nz), jnp.float32),
            pltpu.VMEM((chunks, slab * ny, CHUNK, nz), jnp.bfloat16),
            pltpu.VMEM(held, jnp.bfloat16),
            dma((chunks, GROUP - 1)), dma((chunks, GROUP - 1)),
            dma((GROUP - 1,)), dma((GROUP - 1,)),
            dma((3, chunks, 2)), dma((3, chunks, 2)),
            dma((chunks, others)), dma((chunks, others)),
            dma((3 * chunks + 2,)),
        ],
        compiler_params=pltpu.CompilerParams(
            collective_id=0, has_side_effects=True, vmem_limit_bytes=56 * 2**20
        ),
        name="filter_and_gram",
    )(orbitals, potential, band_matrix(8, ny), band_matrix(1, nz))


def rotate_kernel(counts, early, first_ref, *refs):
    refs, (out_ref, wide) = refs[:-2], refs[-2:]
    orbs = out_ref.shape[0]
    all_rows = wide.shape[0] // orbs
    taken = 0
    for at, count in enumerate(counts):
        weight, parts = refs[taken], refs[taken + 1 : taken + 1 + count]
        taken += 1 + count
        rows, chunk, nz = parts[0].shape[1:]
        start = first_ref[at]

        def body(i, _, weight=weight, parts=parts, start=start, chunk=chunk, nz=nz):
            def orbitals_at(row):
                return jnp.concatenate(
                    [part[:, row].reshape(part.shape[0] * chunk, nz) for part in parts], axis=0
                )

            x = jnp.concatenate([orbitals_at(2 * i), orbitals_at(2 * i + 1)], axis=1)
            y = jnp.dot(weight[...], x, preferred_element_type=jnp.float32)
            for h in range(2):
                wide[pl.ds(start + 2 * i + h, orbs, stride=all_rows), :] = y[:, h * nz : (h + 1) * nz]
            return 0

        lax.fori_loop(0, rows // 2, body, 0)

    def narrow(i, _):
        part = wide[pl.ds(pl.multiple_of(i * 8 * all_rows, 8 * all_rows), 8 * all_rows), :]
        part = part.reshape(8, all_rows, -1).astype(jnp.bfloat16)
        if early:
            some = pl.ds(i * 8, 8)
            out_ref[some, pl.ds(pl.multiple_of(first_ref[len(counts)], all_rows), all_rows)] = part
            at = pl.multiple_of(first_ref[len(counts) + 1], all_rows)
            out_ref[some, pl.ds(at, all_rows)] = refs[-1][some]
        else:
            out_ref[pl.ds(i * 8, 8)] = part
        return 0

    lax.fori_loop(0, orbs // 8, narrow, 0)


def rotate(pieces, firsts, all_rows, early=None):
    orbs = pieces[0][0].shape[0]
    nz = pieces[0][1].shape[3]
    vmem = pl.BlockSpec(memory_space=pltpu.VMEM)
    operands = [array for piece in pieces for array in piece]
    made = all_rows
    if early is not None:
        operands.append(early)
        made -= early.shape[1]
    return pl.pallas_call(
        functools.partial(
            rotate_kernel, [len(piece) - 1 for piece in pieces], early is not None
        ),
        out_shape=jax.ShapeDtypeStruct((orbs, all_rows, nz), jnp.bfloat16),
        in_specs=[pl.BlockSpec(memory_space=pltpu.SMEM)] + [vmem] * len(operands),
        out_specs=vmem,
        scratch_shapes=[pltpu.VMEM((orbs * made, nz), jnp.float32)],
        compiler_params=pltpu.CompilerParams(vmem_limit_bytes=48 * 2**20),
        name="rotate",
    )(firsts, *operands)


def sum_kernel(bands, doms, scale, part_ref, out_ref, near, far, whole, *sems):
    near_send, near_recv, far_send, far_recv, all_send, all_recv = sems
    size = part_ref.shape[0]
    members = GROUP * bands
    rows = size // members
    z_count = doms // GROUP
    b, d = lax.axis_index("band"), lax.axis_index("dom")
    g, z = lax.rem(d, GROUP), d // GROUP
    others = [(k, j) for k in range(GROUP) for j in range(bands) if k or j]

    def place(k, j):
        return lax.rem(g + k, GROUP), lax.rem(b + j, bands)

    def near_device(k, j):
        to_g, to_b = place(k, j)
        return (to_b, z * GROUP + to_g)

    def far_device(h):
        return (b, lax.rem(z + h, z_count) * GROUP + g)

    def block(to_g, to_b):
        return pl.ds(pl.multiple_of((to_g * bands + to_b) * rows, rows), rows)

    barrier = pltpu.get_barrier_semaphore()
    for k, j in others:
        pl.semaphore_signal(barrier, inc=1, device_id=near_device(k, j), device_id_type=MESH)
    for h in range(1, z_count):
        pl.semaphore_signal(barrier, inc=1, device_id=far_device(h), device_id_type=MESH)
    pl.semaphore_wait(barrier, members - 1 + z_count - 1)

    copies = []
    for at, (k, j) in enumerate(others):
        copy = pltpu.make_async_remote_copy(
            part_ref.at[block(*place(k, j))], near.at[at], near_send.at[at], near_recv.at[at],
            device_id=near_device(k, j), device_id_type=MESH,
        )
        copy.start()
        copies.append(copy)
    total = part_ref[block(g, b), :]
    for at, copy in enumerate(copies):
        copy.wait_recv()
        total = total + near[at]
    far[z] = total
    for h in range(1, z_count):
        copy = pltpu.make_async_remote_copy(
            far.at[z], far.at[z], far_send.at[h - 1], far_recv.at[h - 1],
            device_id=far_device(h), device_id_type=MESH,
        )
        copy.start()
        copies.append(copy)
    for copy in copies[len(others):]:
        copy.wait_recv()
    total = far[0]
    for h in range(1, z_count):
        total = total + far[h]
    own = block(g, b)
    whole[own, :] = total * scale
    last = []
    for at, (k, j) in enumerate(others):
        copy = pltpu.make_async_remote_copy(
            whole.at[own], whole.at[own], all_send.at[at], all_recv.at[at],
            device_id=near_device(k, j), device_id_type=MESH,
        )
        copy.start()
        last.append(copy)
    for copy in last:
        copy.wait_recv()
    out_ref[...] = whole[...]
    for copy in copies + last:
        copy.wait_send()


def sum_everywhere(part, bands, doms, scale):
    size, width = part.shape
    others = GROUP * bands - 1
    z_count = doms // GROUP
    rows = size // (GROUP * bands)
    dma = pltpu.SemaphoreType.DMA
    vmem = pl.BlockSpec(memory_space=pltpu.VMEM)
    far = max(z_count - 1, 1)
    return pl.pallas_call(
        functools.partial(sum_kernel, bands, doms, scale),
        out_shape=jax.ShapeDtypeStruct(part.shape, jnp.float32),
        in_specs=[vmem],
        out_specs=vmem,
        scratch_shapes=[
            pltpu.VMEM((others, rows, width), jnp.float32),
            pltpu.VMEM((z_count, rows, width), jnp.float32),
            pltpu.VMEM(part.shape, jnp.float32),
            dma((others,)), dma((others,)), dma((far,)), dma((far,)), dma((others,)), dma((others,)),
        ],
        compiler_params=pltpu.CompilerParams(
            collective_id=1, has_side_effects=True, vmem_limit_bytes=16 * 2**20
        ),
        name="sum_everywhere",
    )(part)


PIVOTS = 4


def eliminate(diag, low, i, _):
    first = low + i * PIVOTS
    held = diag[low:, :]
    row_id = lax.broadcasted_iota(jnp.int32, held.shape, 0) + low
    lane_id = lax.broadcasted_iota(jnp.int32, held.shape, 1)
    one_row = lax.broadcasted_iota(jnp.int32, (1, BLOCK), 1)
    rows = [diag[pl.ds(first + p, 1), :] for p in range(PIVOTS)]

    def pick(p, q):
        return jnp.sum(jnp.where(one_row == first + q, rows[p], 0.0), axis=1, keepdims=True)

    corner = [[pick(p, q) if q >= p else None for q in range(PIVOTS)] for p in range(PIVOTS)]
    columns = [
        jnp.sum(jnp.where(lane_id == first + p, held, 0.0), axis=1, keepdims=True)
        for p in range(PIVOTS)
    ]
    roots, lower = [], [[None] * PIVOTS for _ in range(PIVOTS)]
    for p in range(PIVOTS):
        pivot = corner[p][p]
        root = lax.rsqrt(pivot)
        root = root * (1.5 - 0.5 * pivot * root * root)
        roots.append(root)
        for q in range(p + 1, PIVOTS):
            lower[q][p] = corner[p][q] * root
        for q in range(p + 1, PIVOTS):
            for t in range(q, PIVOTS):
                corner[q][t] = corner[q][t] - lower[q][p] * lower[t][p]
    inside = (one_row >= first) & (one_row < first + PIVOTS)
    rest = jnp.where((lane_id >= first) & (lane_id < first + PIVOTS), 0.0, held)
    scaled, factors = [], []
    for p in range(PIVOTS):
        row = jnp.where(one_row == first + p, 1.0, jnp.where(inside, 0.0, rows[p]))
        column = columns[p]
        for t in range(p):
            row = row - lower[p][t] * scaled[t]
            column = column - factors[t] * lower[p][t]
        scaled.append(row * roots[p])
        factors.append(column * roots[p])
        rest = rest - factors[p] * scaled[p]
    diag[low:, :] = jnp.where(row_id >= first + PIVOTS, rest, held)
    for p in range(PIVOTS):
        diag[pl.ds(first + p, 1), :] = scaled[p]
    return 0


def inverse_factor_kernel(gram_ref, out_ref, full, diag):
    size = full.shape[0]
    exact = lax.Precision.HIGHEST
    for at, (i, j) in enumerate(lower_blocks(size)):
        rows, lanes = slice(i * BLOCK, (i + 1) * BLOCK), slice(j * BLOCK, (j + 1) * BLOCK)
        tile = gram_ref[at * BLOCK : (at + 1) * BLOCK, :]
        full[rows, lanes] = tile
        if i != j:
            full[lanes, rows] = tile.T
    row_id = lax.broadcasted_iota(jnp.int32, (BLOCK, BLOCK), 0)
    lane_id = lax.broadcasted_iota(jnp.int32, (BLOCK, BLOCK), 1)
    for first in range(0, size, BLOCK):
        here, after = slice(first, first + BLOCK), first + BLOCK
        diag[...] = full[here, here]

        for low in range(0, BLOCK, BLOCK // 4):
            eliminate_from = functools.partial(eliminate, diag, low)
            lax.fori_loop(0, BLOCK // 4 // PIVOTS, eliminate_from, 0)
        inverse = jnp.where(row_id >= lane_id, diag[...], 0.0)
        if first:
            full[here, :first] = jnp.dot(
                inverse, full[here, :first], precision=exact, preferred_element_type=jnp.float32
            )
        full[here, here] = inverse
        if after < size:
            upper = jnp.dot(
                inverse, full[here, after:], precision=exact, preferred_element_type=jnp.float32
            )
            full[here, after:] = upper
            full[after:, here] = jnp.zeros((size - after, BLOCK), jnp.float32)
            full[after:, :] -= lax.dot_general(
                upper, full[here, :], (((0,), (0,)), ((), ())),
                precision=exact, preferred_element_type=jnp.float32,
            )
    row_all = lax.broadcasted_iota(jnp.int32, (size, size), 0)
    lane_all = lax.broadcasted_iota(jnp.int32, (size, size), 1)
    out_ref[...] = jnp.where(row_all >= lane_all, full[...], 0.0).astype(jnp.bfloat16)


def rotation_from(gram, size):
    vmem = pl.BlockSpec(memory_space=pltpu.VMEM)
    return pl.pallas_call(
        inverse_factor_kernel,
        out_shape=jax.ShapeDtypeStruct((size, size), jnp.bfloat16),
        in_specs=[vmem],
        out_specs=vmem,
        scratch_shapes=[
            pltpu.VMEM((size, size), jnp.float32), pltpu.VMEM((BLOCK, BLOCK), jnp.float32)
        ],
        compiler_params=pltpu.CompilerParams(vmem_limit_bytes=16 * 2**20),
        cost_estimate=pl.CostEstimate(
            flops=40 * size**3, bytes_accessed=100 * 2**20, transcendentals=0
        ),
        name="inverse_factor",
    )(gram)


def local(bands, doms, orbitals, potential):
    orbs, planes, ny, nz = orbitals.shape
    all_rows = planes * ny
    total_cells = all_rows * nz * doms
    part, held, kept = filter_and_gram(orbitals, potential, bands, doms)
    gram = sum_everywhere(part, bands, doms, 1.0 / total_cells)
    gram, held, kept = lax.optimization_barrier((gram, held, kept))
    b, d = lax.axis_index("band"), lax.axis_index("dom")
    rows_part = all_rows // bands
    if bands == 2:
        g = d % GROUP
        share = orbs // GROUP
        count = orbs // CHUNK
        partner = lax.dynamic_slice_in_dim(held, b * count, count, 0)
        partner = lax.ppermute(partner, "band", [(0, 1), (1, 0)])
        near = []
        for k in range(GROUP):
            row = (g + k) % GROUP * all_rows + (1 - b) * rows_part
            piece = lax.dynamic_slice_in_dim(kept, row, rows_part, 1)
            if k:
                ring = [(i, i // GROUP * GROUP + (i + k) % GROUP) for i in range(doms)]
                piece = lax.ppermute(piece, "dom", ring)
            near.append(piece)
    else:
        rings = [[((i + j) % bands, i) for i in range(bands)] for j in range(1, bands)]
        others = [lax.ppermute(held, "band", ring) for ring in rings]
    rotation = rotation_from(gram, bands * orbs)
    own_rows = lax.dynamic_slice_in_dim(rotation, b * orbs, orbs, 0)
    pieces = [[own_rows, held]]
    if bands == 2:
        starts = [b * orbs + (g - k) % GROUP * share for k in range(GROUP)]
        columns = [lax.dynamic_slice_in_dim(own_rows, start, share, 1) for start in starts]
        columns.append(lax.dynamic_slice_in_dim(own_rows, (1 - b) * orbs, orbs, 1))
        early = rotate(pieces, jnp.zeros((1,), jnp.int32), rows_part)
        pieces = [[jnp.concatenate(columns, axis=1), *near, partner]]
        places = jnp.stack([jnp.zeros_like(b), (1 - b) * rows_part, b * rows_part])
        result = rotate(pieces, places.astype(jnp.int32), all_rows, early)
    else:
        pieces += [[own_rows, other] for other in others]
        firsts = (b + jnp.arange(bands, dtype=jnp.int32)) % bands * rows_part
        result = rotate(pieces, firsts.astype(jnp.int32), all_rows)
    return result.reshape(orbitals.shape)


def solution(mesh):
    placed = (P("band", "dom", None, None), P("dom", None, None))
    return jax.shard_map(
        functools.partial(local, mesh.shape["band"], mesh.shape["dom"]),
        mesh=mesh, in_specs=placed, out_specs=P("band", "dom", None, None), check_vma=False,
    )
```
